32 devices in a mesh: lat: 8 (over z, core), freq: 4 (over y, x).
Axes of the slice: x: 2, y: 2, z: 4, core: 2. Of those that a mesh axis runs over, the one named last changes fastest.
Arguments:
- wavefield: float32 [2, 8, 2048, 2048], P(None, 'freq', 'lat'), may hold values from -6 to 6
- source_field: float32 [2, 8, 2048, 2048], P(None, 'freq', 'lat'), may hold values from -6 to 6
- slowness: float32 [2048, 2048], P('lat', 'freq'), may hold values from 0.00015 to 0.00094
- freq_index: int32 [8], P('freq'), may hold values from 192 to 767, as said below
Outputs:
- next_field: float32 [2, 8, 2048, 2048], P(None, 'freq', 'lat')
- image: float32 [2048, 2048], P('lat', 'freq')
The draws below stay inside these ranges and needn't reach their ends.
Inputs may be any that keep to these rules, and one draw needn't show every extreme that they name: `freq_index`: distinct frequency indices.
All inputs are finite; a program needn't handle non-finite values.
Results may differ from the reference program's by a relative error of at most 0.00013.
Values sent between devices are 32-bit elements; how exact they have to be, the bound alone decides.
A program may use at most 128 MiB of HBM per device.

```python
import math
import jax
import jax.numpy as jnp
from jax import lax

NX = 2048
NY = 2048
BATCH = 8


def draw_slowness(key, part):
    rows = jnp.arange(NX, dtype=jnp.float32)[:, None] / (NX - 1)
    base = 1.0 / 4500.0 * (1.0 + 2.0 * rows)
    rough = jnp.exp(jax.random.uniform(key, (NX, NY), jnp.float32, jnp.log(0.7), jnp.log(1.4)))
    return base * rough


def draw_freq_index(key, part):
    first_key = jax.random.fold_in(key, 11)
    second_key = jax.random.fold_in(key, 23)
    middle = jax.random.permutation(first_key, 574)[:BATCH - 2] + 193
    values = jnp.concatenate([jnp.array([192, 767], jnp.int32), middle.astype(jnp.int32)])
    return jax.random.permutation(second_key, values).astype(jnp.int32)


def shard_levels(stream_key, shape, split, smallest, high):
    factor_of = 1.0
    for axis_at, blocks in split:
        heights = jax.random.uniform(jax.random.fold_in(jax.random.fold_in(stream_key, 6), axis_at), (blocks,), jnp.float32, smallest / len(split), high / len(split))
        factor_of = factor_of * jnp.repeat(jnp.exp(heights), shape[axis_at] // blocks).reshape((-1,) + (1,) * (len(shape) - 1 - axis_at))
    return factor_of


def noise(stream_key, extent, width, reach, shards=(), kind=jnp.bfloat16):
    level = shard_levels(stream_key, extent, shards, -0.22, 0.18) if shards else 1.0
    drawn = jax.random.normal(stream_key, extent, jnp.float32) * width * level
    return jnp.minimum(jnp.maximum(drawn, -reach), reach).astype(kind)


def setup_inputs(seed: int = 0) -> dict:
    streams_of = jax.random.split(jax.random.key(seed), 5)
    wavefield = noise(streams_of[0], (2, BATCH, NX, NY), 1.0, 6.0, ((1, 4), (2, 8)), jnp.float32)
    source_field = noise(streams_of[1], (2, BATCH, NX, NY), 1.0, 6.0, ((1, 4), (2, 8)), jnp.float32)
    slowness = draw_slowness(jax.random.fold_in(streams_of[4], 71), 0)
    freq_index = draw_freq_index(jax.random.fold_in(streams_of[4], 71), 0)
    return dict(wavefield=wavefield, source_field=source_field, slowness=slowness, freq_index=freq_index)


depth_step = 10.0
grid_step = 25.0
freq_step = 0.0625

def wave_numbers(count, float_type):
    indices = jnp.arange(count, dtype=jnp.int32)
    signed = jnp.where(indices < count // 2, indices, indices - count)
    return 2.0 * math.pi / (count * grid_step) * signed.astype(float_type)

def laplace_field(field):
    padded = jnp.pad(field, ((0, 0), (1, 1), (1, 1)))
    beside_all = padded[:, 2:, 1:-1] + padded[:, :-2, 1:-1] + padded[:, 1:-1, 2:] + padded[:, 1:-1, :-2]
    return beside_all - 4.0 * field

def reference(wavefield, source_field, slowness, freq_index):
    float_type = wavefield.dtype
    mean_slow = jnp.mean(slowness)
    angular = 2.0 * math.pi * freq_step * freq_index.astype(float_type)
    field = lax.complex(wavefield[0], wavefield[1])
    lens_angle = angular[:, None, None] * (slowness - mean_slow)[None] * depth_step
    field = field * lax.complex(jnp.cos(lens_angle), jnp.sin(lens_angle))
    spectrum = jnp.fft.fft2(field, axes=(1, 2))
    wave_x = wave_numbers(NX, float_type)
    wave_y = wave_numbers(NY, float_type)
    vertical = (angular * mean_slow)[:, None, None] ** 2 - wave_x[None, :, None] ** 2 - wave_y[None, None, :] ** 2
    damping = jnp.exp(-jnp.sqrt(jnp.maximum(-vertical, 0.0)) * depth_step)
    advance = jnp.sqrt(jnp.maximum(vertical, 0.0)) * depth_step
    spectrum = spectrum * lax.complex(damping * jnp.cos(advance), damping * jnp.sin(advance))
    field = jnp.fft.ifft2(spectrum, axes=(1, 2))
    real_part = jnp.real(field)
    imag_part = jnp.imag(field)
    lateral_gain = depth_step * (0.5 / (angular[:, None, None] * mean_slow) - 0.5 / (angular[:, None, None] * slowness[None])) / (grid_step * grid_step)
    new_real = real_part + lateral_gain * laplace_field(imag_part)
    new_imag = imag_part - lateral_gain * laplace_field(real_part)
    image = lax.optimization_barrier(jnp.sum(new_real * source_field[0] + new_imag * source_field[1], axis=0)) / math.sqrt(BATCH)
    return (jnp.stack([new_real, new_imag]), image)
```

```python
import functools
import math

import jax
import jax.numpy as jnp
import numpy as np
from jax import lax
from jax.experimental import pallas as pl
from jax.experimental.pallas import tpu as pltpu
from jax.sharding import PartitionSpec as P

depth_step = 10.0
grid_step = 25.0
freq_step = 0.0625
LANES = 128
HALO = 8
VMEM_BYTES = 48 * 1024 * 1024


def dft_tables(sign):
    i = np.arange(LANES)
    ang = 2.0 * math.pi / LANES * ((i[:, None] * i[None, :]) % LANES)
    c, s = np.cos(ang), sign * np.sin(ang)
    return np.block([[c, s], [-s, c]])


def split_table(table):
    high = jnp.asarray(table.astype(np.float32)).astype(jnp.bfloat16)
    high64 = np.asarray(table.astype(np.float32).astype(jnp.bfloat16)).astype(np.float64)
    low = (table - high64).astype(np.float32).astype(jnp.bfloat16)
    return jnp.stack([high, jnp.asarray(low)])


def twiddle(count):
    factor = count // LANES
    k, n = np.arange(factor), np.arange(LANES)
    ang = 2.0 * math.pi / count * ((k[:, None] * n[None, :]) % count)
    return np.stack([np.cos(ang), np.sin(ang)]).astype(np.float32)


def fft_list(values, sign):
    count = len(values)
    if count == 1:
        return values
    even, odd = fft_list(values[0::2], sign), fft_list(values[1::2], sign)
    low, high = [], []
    for k in range(count // 2):
        (er, ei), (r, i) = even[k], odd[k]
        if k == 0:
            tr, ti = r, i
        elif 4 * k == count:
            tr, ti = (-i, r) if sign > 0 else (i, -r)
        else:
            c = math.cos(2.0 * math.pi * k / count)
            s = sign * math.sin(2.0 * math.pi * k / count)
            if abs(abs(c) - abs(s)) < 1e-9:
                h = math.sqrt(0.5)
                sc, ss = (1 if c > 0 else -1), (1 if s > 0 else -1)
                tr = h * (r - i) if sc * ss > 0 else h * (r + i)
                ti = h * (i + r) if sc * ss > 0 else h * (i - r)
                if sc < 0:
                    tr, ti = -tr, -ti
            else:
                tr, ti = c * r - s * i, c * i + s * r
        low.append((er + tr, ei + ti))
        high.append((er - tr, ei - ti))
    return low + high


def sin_cos(angle):
    turns = jnp.round(angle * (0.5 / math.pi))
    r = angle - turns * 6.28125 - turns * (2.0 * math.pi - 6.28125)
    r2 = r * r
    s = jnp.full_like(r, 1.0 / math.factorial(17))
    for n in range(15, 0, -2):
        s = s * r2 + ((-1) ** (n // 2)) / math.factorial(n)
    c = jnp.full_like(r, -1.0 / math.factorial(18))
    for n in range(16, -1, -2):
        c = c * r2 + ((-1) ** (n // 2)) / math.factorial(n)
    return s * r, c


def split(x):
    high = x.astype(jnp.bfloat16)
    return high, (x - high.astype(jnp.float32)).astype(jnp.bfloat16)


def dot(a, b):
    return jnp.dot(a, b, preferred_element_type=jnp.float32)


def forward_kernel(ang_ref, wave_ref, slow_ref, tw_ref, m_ref, out_ref, zs, *, member):
    factor, block = zs.shape[0], zs.shape[1]
    part_width, width = slow_ref.shape[2], out_ref.shape[3]
    scale = ang_ref[member] * depth_step

    def tile(t, carry):
        rows = pl.ds(pl.multiple_of(t * 8, 8), 8)
        cells = []
        for n in range(factor):
            at = n * LANES
            s = slow_ref[at // part_width, rows, pl.ds(at % part_width, LANES)]
            sn, cs = sin_cos(s * scale)
            re = wave_ref[0, 0, rows, pl.ds(at, LANES)]
            im = wave_ref[1, 0, rows, pl.ds(at, LANES)]
            cells.append((re * cs - im * sn, re * sn + im * cs))
        for k, (re, im) in enumerate(fft_list(cells, -1.0)):
            if k:
                c, s = tw_ref[0, pl.ds(k, 1), :], tw_ref[1, pl.ds(k, 1), :]
                re, im = re * c + im * s, im * c - re * s
            zs[k, rows, pl.ds(0, LANES)] = re
            zs[k, rows, pl.ds(LANES, LANES)] = im
        return carry

    lax.fori_loop(0, block // 8, tile, 0)
    for g in range(0, factor, 4):
        high, low = split(zs[pl.ds(g, 4)].reshape(4 * block, 2 * LANES))
        y = dot(high, m_ref[0]) + (dot(low, m_ref[0]) + dot(high, m_ref[1]))
        y = y.reshape(4, block, 2 * LANES)
        for j in range(4):
            at = (g + j) * LANES
            cols = pl.ds(at % width, LANES)
            out_ref[at // width, 0, :, cols] = y[j, :, :LANES]
            out_ref[at // width, 1, :, cols] = y[j, :, LANES:]


def shift_kernel(ang_ref, mean_ref, in_ref, tw_ref, m_ref, out_ref, zs, *, member):
    factor, width = zs.shape[0], zs.shape[2]
    strips, rows_in = in_ref.shape[0], in_ref.shape[2]
    count = factor * LANES
    base = lax.axis_index("lat") * width

    def tile_in(t, carry):
        r = pl.multiple_of(t * 8, 8)
        for lane in range(0, width, LANES):
            lanes = pl.ds(lane, LANES)
            cells = []
            for n in range(factor):
                at = n * LANES
                rows = pl.ds(at % rows_in + r, 8)
                cells.append(
                    (in_ref[at // rows_in, 0, rows, lanes], in_ref[at // rows_in, 1, rows, lanes])
                )
            for k, (re, im) in enumerate(fft_list(cells, -1.0)):
                if k:
                    c, s = tw_ref[0, k, pl.ds(r, 8), :], tw_ref[1, k, pl.ds(r, 8), :]
                    re, im = re * c + im * s, im * c - re * s
                zs[k, pl.ds(r, 8), lanes] = re
                zs[k, pl.ds(LANES + r, 8), lanes] = im
        return carry

    lax.fori_loop(0, LANES // 8, tile_in, 0)

    flat = angular_mean = ang_ref[member] * mean_ref[0]
    flat = angular_mean * depth_step
    place = base + lax.broadcasted_iota(jnp.int32, (LANES, width), 1)
    index_y = place // LANES + factor * (place % LANES)
    signed_y = jnp.where(index_y < count // 2, index_y, index_y - count)
    wave_y = 2.0 * math.pi / (count * grid_step) * signed_y.astype(jnp.float32)
    rest = angular_mean * angular_mean - wave_y * wave_y
    row = lax.broadcasted_iota(jnp.int32, (LANES, width), 0)

    def product(k, carry):
        high, low = split(zs[k])
        y = dot(m_ref[0], high) + (dot(m_ref[0], low) + dot(m_ref[1], high))
        index_x = k + factor * row
        signed_x = jnp.where(index_x < count // 2, index_x, index_x - count)
        wave_x = 2.0 * math.pi / (count * grid_step) * signed_x.astype(jnp.float32)
        vertical = rest - wave_x * wave_x
        size = jnp.sqrt(jnp.abs(vertical)) * depth_step
        damping = jnp.where(vertical < 0.0, jnp.exp(-size), 1.0) * (1.0 / (count * count))
        sn, cs = sin_cos(jnp.where(vertical > 0.0, size, 0.0) - flat)
        tr, ti = damping * cs, damping * sn
        re, im = y[:LANES], y[LANES:]
        z = jnp.concatenate([re * tr - im * ti, re * ti + im * tr], axis=0)
        high, low = split(z)
        zs[k] = dot(m_ref[2], high) + (dot(m_ref[2], low) + dot(m_ref[3], high))
        return carry

    lax.fori_loop(0, factor, product, 0)

    def tile_out(t, carry):
        r = pl.multiple_of(t * 8, 8)
        for lane in range(0, width, LANES):
            lanes = pl.ds(lane, LANES)
            cells = []
            for k in range(factor):
                re, im = zs[k, pl.ds(r, 8), lanes], zs[k, pl.ds(LANES + r, 8), lanes]
                if k:
                    c, s = tw_ref[0, k, pl.ds(r, 8), :], tw_ref[1, k, pl.ds(r, 8), :]
                    re, im = re * c - im * s, im * c + re * s
                cells.append((re, im))
            for n, (re, im) in enumerate(fft_list(cells, 1.0)):
                at = n * LANES
                rows = pl.ds(at % rows_in + r, 8)
                out_ref[at // rows_in, 0, rows, lanes] = re
                out_ref[at // rows_in, 1, rows, lanes] = im
        return carry

    lax.fori_loop(0, LANES // 8, tile_out, 0)
    for d in range(strips):
        for c in range(2):
            out_ref[d, c, pl.ds(rows_in, HALO), :] = jnp.zeros((HALO, width), jnp.float32)
            if d > 0:
                out_ref[d, c, pl.ds(rows_in, 1), :] = out_ref[d - 1, c, pl.ds(rows_in - 1, 1), :]
            if d < strips - 1:
                out_ref[d, c, pl.ds(rows_in + 1, 1), :] = out_ref[d + 1, c, pl.ds(0, 1), :]


def finish_kernel(
    ang_ref, mean_ref, in_ref, src_ref, slow_ref, tw_ref, m_ref, *rest, member, batch_total
):
    if member:
        _, before_ref, out_ref, term_ref, zs, field = rest
    else:
        out_ref, term_ref, zs, field = rest
    factor, tall = zs.shape[0], zs.shape[1]
    rows_in, width = tall - HALO, in_ref.shape[3]
    block, full = term_ref.shape
    step = pl.program_id(0)

    @pl.when(step == 0)
    def _():
        for k in range(factor):
            at = k * LANES
            cols = pl.ds(at % width, LANES)
            x = jnp.concatenate(
                [in_ref[at // width, 0, :, cols], in_ref[at // width, 1, :, cols]], axis=1
            )
            high, low = split(x)
            zs[k] = dot(high, m_ref[0]) + (dot(low, m_ref[0]) + dot(high, m_ref[1]))

        def columns(rows):
            cells = []
            for k in range(factor):
                re, im = zs[k, rows, pl.ds(0, LANES)], zs[k, rows, pl.ds(LANES, LANES)]
                if k:
                    c, s = tw_ref[0, pl.ds(k, 1), :], tw_ref[1, pl.ds(k, 1), :]
                    re, im = re * c - im * s, im * c + re * s
                cells.append((re, im))
            return fft_list(cells, 1.0)

        def tile(t, carry):
            r = pl.multiple_of(t * 8, 8)
            for n, pair in enumerate(columns(pl.ds(r, 8))):
                for c in range(2):
                    field[c, pl.ds(8 + r, 8), pl.ds(n * LANES, LANES)] = pair[c]
            return carry

        lax.fori_loop(0, rows_in // 8, tile, 0)
        for n, pair in enumerate(columns(pl.ds(rows_in, 8))):
            for c in range(2):
                field[c, pl.ds(7, 1), pl.ds(n * LANES, LANES)] = pair[c][0:1]
                field[c, pl.ds(8 + rows_in, 1), pl.ds(n * LANES, LANES)] = pair[c][1:2]

    angular = ang_ref[member]
    ahead = 0.5 / (angular * mean_ref[0])
    column = lax.broadcasted_iota(jnp.int32, (block, full), 1)
    start = pl.multiple_of(step * block, 8)
    centre, laplace = [], []
    for c in range(2):
        cells = field[c, pl.ds(start, block + 16), :]
        mid = cells[8 : 8 + block]
        up = pltpu.roll(cells, 1, 0)[8 : 8 + block]
        down = pltpu.roll(cells, block + 15, 0)[8 : 8 + block]
        left = jnp.where(column == 0, 0.0, pltpu.roll(mid, 1, 1))
        right = jnp.where(column == full - 1, 0.0, pltpu.roll(mid, full - 1, 1))
        centre.append(mid)
        laplace.append(up + down + left + right - 4.0 * mid)
    slow = jnp.concatenate([slow_ref[p] for p in range(slow_ref.shape[0])], axis=1)
    gain = (ahead - 0.5 / (angular * slow)) * (depth_step / (grid_step * grid_step))
    new_re = centre[0] + gain * laplace[1]
    new_im = centre[1] - gain * laplace[0]
    out_ref[0, 0] = new_re
    out_ref[1, 0] = new_im
    term = (new_re * src_ref[0, 0] + new_im * src_ref[1, 0]) * (1.0 / math.sqrt(batch_total))
    term_ref[...] = term + before_ref[...] if member else term


def params():
    return pltpu.CompilerParams(vmem_limit_bytes=VMEM_BYTES)


def whole(array):
    zeros = (0,) * array.ndim
    return pl.BlockSpec(array.shape, lambda *_: zeros)


SMEM = pl.BlockSpec(memory_space=pltpu.SMEM)


def local(wavefield, source_field, slowness, freq_index):
    _, members, rows, full = wavefield.shape
    strips, groups = lax.axis_size("lat"), lax.axis_size("freq")
    width = full // strips
    factor = full // LANES
    part_width = full // groups
    count_x = rows * strips
    angular = 2.0 * math.pi * freq_step * freq_index.astype(jnp.float32)
    tw = twiddle(full)
    tw_row = jnp.asarray(tw)
    tw_x = jnp.asarray(np.ascontiguousarray(np.broadcast_to(tw[..., None], tw.shape + (LANES,))))
    right_fwd, right_inv = dft_tables(-1.0), dft_tables(1.0)
    m_fwd, m_inv = split_table(right_fwd), split_table(right_inv)
    m_both = jnp.concatenate(
        [split_table(np.ascontiguousarray(right_fwd.T)), split_table(np.ascontiguousarray(right_inv.T))]
    )
    strip = lax.all_gather(slowness, "freq", axis=0, tiled=False)

    block = 64

    def forward(member):
        return pl.pallas_call(
            functools.partial(forward_kernel, member=member),
            grid=(rows // block,),
            in_specs=[
                SMEM,
                pl.BlockSpec((2, 1, block, full), lambda i: (0, member, i, 0)),
                pl.BlockSpec((groups, block, part_width), lambda i: (0, i, 0)),
                whole(tw_row),
                whole(m_fwd),
            ],
            out_specs=pl.BlockSpec((strips, 2, block, width), lambda i: (0, 0, i, 0)),
            out_shape=jax.ShapeDtypeStruct((strips, 2, rows, width), jnp.float32),
            scratch_shapes=[pltpu.VMEM((factor, block, 2 * LANES), jnp.float32)],
            compiler_params=params(),
            cost_estimate=pl.CostEstimate(
                flops=4_000_000_000, bytes_accessed=40_000_000, transcendentals=0
            ),
            name="forward",
        )(angular, wavefield, strip, tw_row, m_fwd)

    def shift(member, mean_slow, spectra):
        return pl.pallas_call(
            functools.partial(shift_kernel, member=member),
            grid=(1,),
            in_specs=[SMEM, SMEM, whole(spectra), whole(tw_x), whole(m_both)],
            out_specs=pl.BlockSpec((strips, 2, rows + HALO, width), lambda i: (0, 0, 0, 0)),
            out_shape=jax.ShapeDtypeStruct((strips, 2, rows + HALO, width), jnp.float32),
            scratch_shapes=[pltpu.VMEM((factor, 2 * LANES, width), jnp.float32)],
            compiler_params=params(),
            cost_estimate=pl.CostEstimate(
                flops=10_000_000_000, bytes_accessed=100_000_000, transcendentals=0
            ),
            name="shift",
        )(angular, mean_slow, spectra, tw_x, m_both)

    final_block = 32

    def finish(member, mean_slow, lines, before):
        strip_block = pl.BlockSpec((groups, final_block, part_width), lambda i: (0, i, 0))
        term_block = pl.BlockSpec((final_block, full), lambda i: (i, 0))
        field_block = pl.BlockSpec((2, 1, final_block, full), lambda i: (0, member, i, 0))
        specs = [SMEM, SMEM, whole(lines), field_block, strip_block, whole(tw_row), whole(m_inv)]
        arrays = [angular, mean_slow, lines, source_field, strip, tw_row, m_inv]
        aliases = {}
        if member:
            aliases = {len(arrays): 0}
            specs += [pl.BlockSpec(memory_space=pl.ANY), term_block]
            arrays += list(before)
        return pl.pallas_call(
            functools.partial(
                finish_kernel, member=member, batch_total=members * groups
            ),
            grid=(rows // final_block,),
            in_specs=specs,
            out_specs=[field_block, term_block],
            out_shape=[
                jax.ShapeDtypeStruct((2, members, rows, full), jnp.float32),
                jax.ShapeDtypeStruct((rows, full), jnp.float32),
            ],
            scratch_shapes=[
                pltpu.VMEM((factor, rows + HALO, 2 * LANES), jnp.float32),
                pltpu.VMEM((2, rows + 16, full), jnp.float32),
            ],
            input_output_aliases=aliases,
            compiler_params=params(),
            cost_estimate=pl.CostEstimate(
                flops=8_000_000_000, bytes_accessed=80_000_000, transcendentals=0
            ),
            name="finish",
        )(*arrays)

    def exchange(cells):
        return lax.all_to_all(cells, "lat", split_axis=0, concat_axis=0, tiled=True)

    spectra = [forward(m) for m in range(members)]
    later, spectra[-1] = lax.optimization_barrier((slowness, spectra[-1]))
    total = lax.psum(jnp.sum(later), ("lat", "freq"))
    mean_slow = (total / (count_x * full)).reshape(1)
    lines = [exchange(s) for s in spectra]
    shifted = [exchange(shift(m, mean_slow, lines[m])) for m in range(members)]
    state = None
    for m in range(members):
        state = finish(m, mean_slow, shifted[m], state)
    field, terms = state
    image = lax.psum_scatter(terms, "freq", scatter_dimension=1, tiled=True)
    return (field, image)


def solution(mesh):
    return jax.shard_map(
        local,
        mesh=mesh,
        in_specs=(
            P(None, "freq", "lat", None),
            P(None, "freq", "lat", None),
            P("lat", "freq"),
            P("freq"),
        ),
        out_specs=(P(None, "freq", "lat", None), P("lat", "freq")),
        check_vma=False,
    )
```

```python
import functools
import math

import jax
import jax.numpy as jnp
import numpy as np
from jax import lax
from jax.experimental import pallas as pl
from jax.experimental.pallas import tpu as pltpu
from jax.sharding import PartitionSpec as P

depth_step = 10.0
grid_step = 25.0
freq_step = 0.0625
LANES = 128
HALO = 8
VMEM_BYTES = 48 * 1024 * 1024


def dft_tables(sign):
    i = np.arange(LANES)
    ang = 2.0 * math.pi / LANES * ((i[:, None] * i[None, :]) % LANES)
    c, s = np.cos(ang), sign * np.sin(ang)
    return np.block([[c, s], [-s, c]])


def split_table(table):
    high = jnp.asarray(table.astype(np.float32)).astype(jnp.bfloat16)
    high64 = np.asarray(table.astype(np.float32).astype(jnp.bfloat16)).astype(np.float64)
    low = (table - high64).astype(np.float32).astype(jnp.bfloat16)
    return jnp.stack([high, jnp.asarray(low)])


def twiddle(count):
    factor = count // LANES
    k, n = np.arange(factor), np.arange(LANES)
    ang = 2.0 * math.pi / count * ((k[:, None] * n[None, :]) % count)
    return np.stack([np.cos(ang), np.sin(ang)]).astype(np.float32)


def fft_list(values, sign):
    count = len(values)
    if count == 1:
        return values
    even, odd = fft_list(values[0::2], sign), fft_list(values[1::2], sign)
    low, high = [], []
    for k in range(count // 2):
        (er, ei), (r, i) = even[k], odd[k]
        if k == 0:
            tr, ti = r, i
        elif 4 * k == count:
            tr, ti = (-i, r) if sign > 0 else (i, -r)
        else:
            c = math.cos(2.0 * math.pi * k / count)
            s = sign * math.sin(2.0 * math.pi * k / count)
            if abs(abs(c) - abs(s)) < 1e-9:
                h = math.sqrt(0.5)
                sc, ss = (1 if c > 0 else -1), (1 if s > 0 else -1)
                tr = h * (r - i) if sc * ss > 0 else h * (r + i)
                ti = h * (i + r) if sc * ss > 0 else h * (i - r)
                if sc < 0:
                    tr, ti = -tr, -ti
            else:
                tr, ti = c * r - s * i, c * i + s * r
        low.append((er + tr, ei + ti))
        high.append((er - tr, ei - ti))
    return low + high


def sin_cos(angle):
    turns = jnp.round(angle * (0.5 / math.pi))
    r = angle - turns * 6.28125 - turns * (2.0 * math.pi - 6.28125)
    r2 = r * r
    s = jnp.full_like(r, 1.0 / math.factorial(17))
    for n in range(15, 0, -2):
        s = s * r2 + ((-1) ** (n // 2)) / math.factorial(n)
    c = jnp.full_like(r, -1.0 / math.factorial(18))
    for n in range(16, -1, -2):
        c = c * r2 + ((-1) ** (n // 2)) / math.factorial(n)
    return s * r, c


def split(x):
    high = x.astype(jnp.bfloat16)
    return high, (x - high.astype(jnp.float32)).astype(jnp.bfloat16)


def dot(a, b):
    return jnp.dot(a, b, preferred_element_type=jnp.float32)


def forward_kernel(ang_ref, wave_ref, slow_ref, tw_ref, m_ref, out_ref, zs, *, member):
    factor, block = zs.shape[0], zs.shape[1]
    part_width, width = slow_ref.shape[2], out_ref.shape[3]
    scale = ang_ref[member] * depth_step

    def tile(t, carry):
        rows = pl.ds(pl.multiple_of(t * 8, 8), 8)
        cells = []
        for n in range(factor):
            at = n * LANES
            s = slow_ref[at // part_width, rows, pl.ds(at % part_width, LANES)]
            sn, cs = sin_cos(s * scale)
            re = wave_ref[0, 0, rows, pl.ds(at, LANES)]
            im = wave_ref[1, 0, rows, pl.ds(at, LANES)]
            cells.append((re * cs - im * sn, re * sn + im * cs))
        for k, (re, im) in enumerate(fft_list(cells, -1.0)):
            if k:
                c, s = tw_ref[0, pl.ds(k, 1), :], tw_ref[1, pl.ds(k, 1), :]
                re, im = re * c + im * s, im * c - re * s
            zs[k, rows, pl.ds(0, LANES)] = re
            zs[k, rows, pl.ds(LANES, LANES)] = im
        return carry

    lax.fori_loop(0, block // 8, tile, 0)
    for g in range(0, factor, 4):
        high, low = split(zs[pl.ds(g, 4)].reshape(4 * block, 2 * LANES))
        y = dot(high, m_ref[0]) + (dot(low, m_ref[0]) + dot(high, m_ref[1]))
        y = y.reshape(4, block, 2 * LANES)
        for j in range(4):
            at = (g + j) * LANES
            cols = pl.ds(at % width, LANES)
            out_ref[at // width, 0, :, cols] = y[j, :, :LANES]
            out_ref[at // width, 1, :, cols] = y[j, :, LANES:]


def shift_kernel(ang_ref, mean_ref, in_ref, tw_ref, m_ref, out_ref, zs, *, member):
    factor, width = zs.shape[0], zs.shape[2]
    strips, rows_in = in_ref.shape[0], in_ref.shape[2]
    count = factor * LANES
    base = lax.axis_index("lat") * width

    def tile_in(t, carry):
        r = pl.multiple_of(t * 8, 8)
        for lane in range(0, width, LANES):
            lanes = pl.ds(lane, LANES)
            cells = []
            for n in range(factor):
                at = n * LANES
                rows = pl.ds(at % rows_in + r, 8)
                cells.append(
                    (in_ref[at // rows_in, 0, rows, lanes], in_ref[at // rows_in, 1, rows, lanes])
                )
            for k, (re, im) in enumerate(fft_list(cells, -1.0)):
                if k:
                    c, s = tw_ref[0, k, pl.ds(r, 8), :], tw_ref[1, k, pl.ds(r, 8), :]
                    re, im = re * c + im * s, im * c - re * s
                zs[k, pl.ds(r, 8), lanes] = re
                zs[k, pl.ds(LANES + r, 8), lanes] = im
        return carry

    lax.fori_loop(0, LANES // 8, tile_in, 0)

    angular_mean = ang_ref[member] * mean_ref[0]
    flat = angular_mean * depth_step
    place = base + lax.broadcasted_iota(jnp.int32, (LANES, width), 1)
    index_y = place // LANES + factor * (place % LANES)
    signed_y = jnp.where(index_y < count // 2, index_y, index_y - count)
    wave_y = 2.0 * math.pi / (count * grid_step) * signed_y.astype(jnp.float32)
    rest = angular_mean * angular_mean - wave_y * wave_y
    row = lax.broadcasted_iota(jnp.int32, (LANES, width), 0)

    def product(k, carry):
        high, low = split(zs[k])
        y = dot(m_ref[0], high) + (dot(m_ref[0], low) + dot(m_ref[1], high))
        index_x = k + factor * row
        signed_x = jnp.where(index_x < count // 2, index_x, index_x - count)
        wave_x = 2.0 * math.pi / (count * grid_step) * signed_x.astype(jnp.float32)
        vertical = rest - wave_x * wave_x
        size = jnp.sqrt(jnp.abs(vertical)) * depth_step
        damping = jnp.where(vertical < 0.0, jnp.exp(-size), 1.0) * (1.0 / (count * count))
        sn, cs = sin_cos(jnp.where(vertical > 0.0, size, 0.0) - flat)
        tr, ti = damping * cs, damping * sn
        re, im = y[:LANES], y[LANES:]
        z = jnp.concatenate([re * tr - im * ti, re * ti + im * tr], axis=0)
        high, low = split(z)
        zs[k] = dot(m_ref[2], high) + (dot(m_ref[2], low) + dot(m_ref[3], high))
        return carry

    lax.fori_loop(0, factor, product, 0)

    def tile_out(t, carry):
        r = pl.multiple_of(t * 8, 8)
        for lane in range(0, width, LANES):
            lanes = pl.ds(lane, LANES)
            cells = []
            for k in range(factor):
                re, im = zs[k, pl.ds(r, 8), lanes], zs[k, pl.ds(LANES + r, 8), lanes]
                if k:
                    c, s = tw_ref[0, k, pl.ds(r, 8), :], tw_ref[1, k, pl.ds(r, 8), :]
                    re, im = re * c - im * s, im * c + re * s
                cells.append((re, im))
            for n, (re, im) in enumerate(fft_list(cells, 1.0)):
                at = n * LANES
                rows = pl.ds(at % rows_in + r, 8)
                out_ref[at // rows_in, 0, rows, lanes] = re
                out_ref[at // rows_in, 1, rows, lanes] = im
        return carry

    lax.fori_loop(0, LANES // 8, tile_out, 0)
    for d in range(strips):
        for c in range(2):
            out_ref[d, c, pl.ds(rows_in, HALO), :] = jnp.zeros((HALO, width), jnp.float32)
            if d > 0:
                out_ref[d, c, pl.ds(rows_in, 1), :] = out_ref[d - 1, c, pl.ds(rows_in - 1, 1), :]
            if d < strips - 1:
                out_ref[d, c, pl.ds(rows_in + 1, 1), :] = out_ref[d + 1, c, pl.ds(0, 1), :]


def finish_kernel(
    ang_ref, mean_ref, in_ref, src_ref, slow_ref, tw_ref, m_ref, *rest, member, batch_total
):
    if member:
        _, before_ref, out_ref, term_ref, zs, field = rest
    else:
        out_ref, term_ref, zs, field = rest
    factor, tall = zs.shape[0], zs.shape[1]
    rows_in, width = tall - HALO, in_ref.shape[3]
    block, part_width = term_ref.shape[1:]
    full = field.shape[2]
    step = pl.program_id(0)

    @pl.when(step == 0)
    def _():
        for k in range(factor):
            at = k * LANES
            cols = pl.ds(at % width, LANES)
            x = jnp.concatenate(
                [in_ref[at // width, 0, :, cols], in_ref[at // width, 1, :, cols]], axis=1
            )
            high, low = split(x)
            zs[k] = dot(high, m_ref[0]) + (dot(low, m_ref[0]) + dot(high, m_ref[1]))

        def columns(rows):
            cells = []
            for k in range(factor):
                re, im = zs[k, rows, pl.ds(0, LANES)], zs[k, rows, pl.ds(LANES, LANES)]
                if k:
                    c, s = tw_ref[0, pl.ds(k, 1), :], tw_ref[1, pl.ds(k, 1), :]
                    re, im = re * c - im * s, im * c + re * s
                cells.append((re, im))
            return fft_list(cells, 1.0)

        def tile(t, carry):
            r = pl.multiple_of(t * 8, 8)
            for n, pair in enumerate(columns(pl.ds(r, 8))):
                for c in range(2):
                    field[c, pl.ds(8 + r, 8), pl.ds(n * LANES, LANES)] = pair[c]
            return carry

        lax.fori_loop(0, rows_in // 8, tile, 0)
        for n, pair in enumerate(columns(pl.ds(rows_in, 8))):
            for c in range(2):
                field[c, pl.ds(7, 1), pl.ds(n * LANES, LANES)] = pair[c][0:1]
                field[c, pl.ds(8 + rows_in, 1), pl.ds(n * LANES, LANES)] = pair[c][1:2]

    angular = ang_ref[member]
    ahead = 0.5 / (angular * mean_ref[0])
    column = lax.broadcasted_iota(jnp.int32, (block, full), 1)
    start = pl.multiple_of(step * block, 8)
    centre, laplace = [], []
    for c in range(2):
        cells = field[c, pl.ds(start, block + 16), :]
        mid = cells[8 : 8 + block]
        up = pltpu.roll(cells, 1, 0)[8 : 8 + block]
        down = pltpu.roll(cells, block + 15, 0)[8 : 8 + block]
        left = jnp.where(column == 0, 0.0, pltpu.roll(mid, 1, 1))
        right = jnp.where(column == full - 1, 0.0, pltpu.roll(mid, full - 1, 1))
        centre.append(mid)
        laplace.append(up + down + left + right - 4.0 * mid)
    slow = jnp.concatenate([slow_ref[p] for p in range(slow_ref.shape[0])], axis=1)
    gain = (ahead - 0.5 / (angular * slow)) * (depth_step / (grid_step * grid_step))
    new_re = centre[0] + gain * laplace[1]
    new_im = centre[1] - gain * laplace[0]
    out_ref[0, 0] = new_re
    out_ref[1, 0] = new_im
    term = (new_re * src_ref[0, 0] + new_im * src_ref[1, 0]) * (1.0 / math.sqrt(batch_total))
    for p in range(slow_ref.shape[0]):
        part = term[:, p * part_width : (p + 1) * part_width]
        term_ref[p] = part + before_ref[p] if member else part


def params():
    return pltpu.CompilerParams(vmem_limit_bytes=VMEM_BYTES)


def whole(array):
    zeros = (0,) * array.ndim
    return pl.BlockSpec(array.shape, lambda *_: zeros)


SMEM = pl.BlockSpec(memory_space=pltpu.SMEM)


def local(wavefield, source_field, slowness, freq_index):
    _, members, rows, full = wavefield.shape
    strips, groups = lax.axis_size("lat"), lax.axis_size("freq")
    width = full // strips
    factor = full // LANES
    part_width = full // groups
    count_x = rows * strips
    angular = 2.0 * math.pi * freq_step * freq_index.astype(jnp.float32)
    tw = twiddle(full)
    tw_row = jnp.asarray(tw)
    tw_x = jnp.asarray(np.ascontiguousarray(np.broadcast_to(tw[..., None], tw.shape + (LANES,))))
    right_fwd, right_inv = dft_tables(-1.0), dft_tables(1.0)
    m_fwd, m_inv = split_table(right_fwd), split_table(right_inv)
    m_both = jnp.concatenate(
        [split_table(np.ascontiguousarray(right_fwd.T)), split_table(np.ascontiguousarray(right_inv.T))]
    )
    total = lax.psum(jnp.sum(slowness), ("lat", "freq"))
    copies = jnp.broadcast_to(slowness, (groups,) + slowness.shape)
    strip = lax.all_to_all(copies, "freq", split_axis=0, concat_axis=0, tiled=True)
    strip, total = lax.optimization_barrier((strip, total))
    mean_slow = (total / (count_x * full)).reshape(1)

    block = 64

    def forward(member):
        return pl.pallas_call(
            functools.partial(forward_kernel, member=member),
            grid=(rows // block,),
            in_specs=[
                SMEM,
                pl.BlockSpec((2, 1, block, full), lambda i: (0, member, i, 0)),
                pl.BlockSpec((groups, block, part_width), lambda i: (0, i, 0)),
                whole(tw_row),
                whole(m_fwd),
            ],
            out_specs=pl.BlockSpec((strips, 2, block, width), lambda i: (0, 0, i, 0)),
            out_shape=jax.ShapeDtypeStruct((strips, 2, rows, width), jnp.float32),
            scratch_shapes=[pltpu.VMEM((factor, block, 2 * LANES), jnp.float32)],
            compiler_params=params(),
            cost_estimate=pl.CostEstimate(
                flops=4_000_000_000, bytes_accessed=40_000_000, transcendentals=0
            ),
            name="forward",
        )(angular, wavefield, strip, tw_row, m_fwd)

    def shift(member, mean_slow, spectra):
        return pl.pallas_call(
            functools.partial(shift_kernel, member=member),
            grid=(1,),
            in_specs=[SMEM, SMEM, whole(spectra), whole(tw_x), whole(m_both)],
            out_specs=pl.BlockSpec((strips, 2, rows + HALO, width), lambda i: (0, 0, 0, 0)),
            out_shape=jax.ShapeDtypeStruct((strips, 2, rows + HALO, width), jnp.float32),
            scratch_shapes=[pltpu.VMEM((factor, 2 * LANES, width), jnp.float32)],
            compiler_params=params(),
            cost_estimate=pl.CostEstimate(
                flops=10_000_000_000, bytes_accessed=100_000_000, transcendentals=0
            ),
            name="shift",
        )(angular, mean_slow, spectra, tw_x, m_both)

    final_block = 32

    def finish(member, mean_slow, lines, before):
        strip_block = pl.BlockSpec((groups, final_block, part_width), lambda i: (0, i, 0))
        field_block = pl.BlockSpec((2, 1, final_block, full), lambda i: (0, member, i, 0))
        specs = [SMEM, SMEM, whole(lines), field_block, strip_block, whole(tw_row), whole(m_inv)]
        arrays = [angular, mean_slow, lines, source_field, strip, tw_row, m_inv]
        aliases = {}
        if member:
            aliases = {len(arrays): 0}
            specs += [pl.BlockSpec(memory_space=pl.ANY), strip_block]
            arrays += list(before)
        return pl.pallas_call(
            functools.partial(
                finish_kernel, member=member, batch_total=members * groups
            ),
            grid=(rows // final_block,),
            in_specs=specs,
            out_specs=[field_block, strip_block],
            out_shape=[
                jax.ShapeDtypeStruct((2, members, rows, full), jnp.float32),
                jax.ShapeDtypeStruct((groups, rows, part_width), jnp.float32),
            ],
            scratch_shapes=[
                pltpu.VMEM((factor, rows + HALO, 2 * LANES), jnp.float32),
                pltpu.VMEM((2, rows + 16, full), jnp.float32),
            ],
            input_output_aliases=aliases,
            compiler_params=params(),
            cost_estimate=pl.CostEstimate(
                flops=8_000_000_000, bytes_accessed=80_000_000, transcendentals=0
            ),
            name="finish",
        )(*arrays)

    def exchange(cells):
        return lax.all_to_all(cells, "lat", split_axis=0, concat_axis=0, tiled=True)

    spectra = [forward(m) for m in range(members)]
    lines = [exchange(s) for s in spectra]
    shifted = [exchange(shift(m, mean_slow, lines[m])) for m in range(members)]
    state = None
    for m in range(members):
        state = finish(m, mean_slow, shifted[m], state)
    field, terms = state
    image = jnp.sum(
        lax.all_to_all(terms, "freq", split_axis=0, concat_axis=0, tiled=True), axis=0
    )
    return (field, image)


def solution(mesh):
    return jax.shard_map(
        local,
        mesh=mesh,
        in_specs=(
            P(None, "freq", "lat", None),
            P(None, "freq", "lat", None),
            P("lat", "freq"),
            P("freq"),
        ),
        out_specs=(P(None, "freq", "lat", None), P("lat", "freq")),
        check_vma=False,
    )
```

```python
import functools
import math

import jax
import jax.numpy as jnp
import numpy as np
from jax import lax
from jax.experimental import pallas as pl
from jax.experimental.pallas import tpu as pltpu
from jax.sharding import PartitionSpec as P

depth_step = 10.0
grid_step = 25.0
freq_step = 0.0625
LANES = 128
HALO = 8
VMEM_BYTES = 48 * 1024 * 1024


def dft_tables(sign):
    i = np.arange(LANES)
    ang = 2.0 * math.pi / LANES * ((i[:, None] * i[None, :]) % LANES)
    c, s = np.cos(ang), sign * np.sin(ang)
    return np.block([[c, s], [-s, c]])


def split_table(table):
    high = jnp.asarray(table.astype(np.float32)).astype(jnp.bfloat16)
    high64 = np.asarray(table.astype(np.float32).astype(jnp.bfloat16)).astype(np.float64)
    low = (table - high64).astype(np.float32).astype(jnp.bfloat16)
    return jnp.stack([high, jnp.asarray(low)])


def twiddle(count):
    factor = count // LANES
    k, n = np.arange(factor), np.arange(LANES)
    ang = 2.0 * math.pi / count * ((k[:, None] * n[None, :]) % count)
    return np.stack([np.cos(ang), np.sin(ang)]).astype(np.float32)


def fft_list(values, sign):
    count = len(values)
    if count == 1:
        return values
    even, odd = fft_list(values[0::2], sign), fft_list(values[1::2], sign)
    low, high = [], []
    for k in range(count // 2):
        (er, ei), (r, i) = even[k], odd[k]
        if k == 0:
            tr, ti = r, i
        elif 4 * k == count:
            tr, ti = (-i, r) if sign > 0 else (i, -r)
        else:
            c = math.cos(2.0 * math.pi * k / count)
            s = sign * math.sin(2.0 * math.pi * k / count)
            if abs(abs(c) - abs(s)) < 1e-9:
                h = math.sqrt(0.5)
                sc, ss = (1 if c > 0 else -1), (1 if s > 0 else -1)
                tr = h * (r - i) if sc * ss > 0 else h * (r + i)
                ti = h * (i + r) if sc * ss > 0 else h * (i - r)
                if sc < 0:
                    tr, ti = -tr, -ti
            else:
                tr, ti = c * r - s * i, c * i + s * r
        low.append((er + tr, ei + ti))
        high.append((er - tr, ei - ti))
    return low + high


def sin_cos(angle):
    turns = jnp.round(angle * (0.5 / math.pi))
    r = angle - turns * 6.28125 - turns * (2.0 * math.pi - 6.28125)
    r2 = r * r
    s = jnp.full_like(r, 1.0 / math.factorial(17))
    for n in range(15, 0, -2):
        s = s * r2 + ((-1) ** (n // 2)) / math.factorial(n)
    c = jnp.full_like(r, -1.0 / math.factorial(18))
    for n in range(16, -1, -2):
        c = c * r2 + ((-1) ** (n // 2)) / math.factorial(n)
    return s * r, c


def split(x):
    high = x.astype(jnp.bfloat16)
    return high, (x - high.astype(jnp.float32)).astype(jnp.bfloat16)


def dot(a, b):
    return jnp.dot(a, b, preferred_element_type=jnp.float32)


def forward_kernel(ang_ref, wave_ref, slow_ref, tw_ref, m_ref, out_ref, zs, total, *, member):
    factor, block = zs.shape[0], zs.shape[1]
    part_width, width = slow_ref.shape[2], out_ref.shape[3]
    scale = ang_ref[member] * depth_step
    step = pl.program_id(0)
    start = pl.multiple_of(step * block, block)
    last = pl.num_programs(0) - 1

    @pl.when(step == 0)
    def _():
        total[...] = jnp.zeros_like(total)

    def tile(t, sums):
        rows = pl.ds(pl.multiple_of(t * 8, 8), 8)
        cells = []
        for n in range(factor):
            at = n * LANES
            s = slow_ref[at // part_width, rows, pl.ds(at % part_width, LANES)]
            sums = sums + s
            sn, cs = sin_cos(s * scale)
            re = wave_ref[0, 0, rows, pl.ds(at, LANES)]
            im = wave_ref[1, 0, rows, pl.ds(at, LANES)]
            cells.append((re * cs - im * sn, re * sn + im * cs))
        for k, (re, im) in enumerate(fft_list(cells, -1.0)):
            if k:
                c, s = tw_ref[0, pl.ds(k, 1), :], tw_ref[1, pl.ds(k, 1), :]
                re, im = re * c + im * s, im * c - re * s
            zs[k, rows, pl.ds(0, LANES)] = re
            zs[k, rows, pl.ds(LANES, LANES)] = im
        return sums

    total[...] = lax.fori_loop(0, block // 8, tile, total[...])
    for g in range(0, factor, 4):
        high, low = split(zs[pl.ds(g, 4)].reshape(4 * block, 2 * LANES))
        y = dot(high, m_ref[0]) + (dot(low, m_ref[0]) + dot(high, m_ref[1]))
        y = y.reshape(4, block, 2 * LANES)
        for j in range(4):
            at = (g + j) * LANES
            cols = pl.ds(at % width, LANES)
            out_ref[at // width, 0, pl.ds(start, block), cols] = y[j, :, :LANES]
            out_ref[at // width, 1, pl.ds(start, block), cols] = y[j, :, LANES:]

    if member == 0:
        @pl.when(step == last)
        def _():
            value = jnp.full((HALO, width), jnp.sum(total[...]), jnp.float32)
            for d in range(out_ref.shape[0]):
                for c in range(2):
                    out_ref[d, c, pl.ds(out_ref.shape[2] - HALO, HALO), :] = value


def shift_kernel(ang_ref, mean_ref, in_ref, tw_ref, m_ref, out_ref, zs, *, member):
    factor, width = zs.shape[0], zs.shape[2]
    strips, rows_in = in_ref.shape[0], out_ref.shape[2] - HALO
    count = factor * LANES
    base = lax.axis_index("lat") * width

    def tile_in(t, carry):
        r = pl.multiple_of(t * 8, 8)
        for lane in range(0, width, LANES):
            lanes = pl.ds(lane, LANES)
            cells = []
            for n in range(factor):
                at = n * LANES
                rows = pl.ds(at % rows_in + r, 8)
                cells.append(
                    (in_ref[at // rows_in, 0, rows, lanes], in_ref[at // rows_in, 1, rows, lanes])
                )
            for k, (re, im) in enumerate(fft_list(cells, -1.0)):
                if k:
                    c, s = tw_ref[0, k, pl.ds(r, 8), :], tw_ref[1, k, pl.ds(r, 8), :]
                    re, im = re * c + im * s, im * c - re * s
                zs[k, pl.ds(r, 8), lanes] = re
                zs[k, pl.ds(LANES + r, 8), lanes] = im
        return carry

    lax.fori_loop(0, LANES // 8, tile_in, 0)

    angular_mean = ang_ref[member] * mean_ref[0]
    flat = angular_mean * depth_step
    place = base + lax.broadcasted_iota(jnp.int32, (LANES, width), 1)
    index_y = place // LANES + factor * (place % LANES)
    signed_y = jnp.where(index_y < count // 2, index_y, index_y - count)
    wave_y = 2.0 * math.pi / (count * grid_step) * signed_y.astype(jnp.float32)
    rest = angular_mean * angular_mean - wave_y * wave_y
    row = lax.broadcasted_iota(jnp.int32, (LANES, width), 0)

    def product(k, carry):
        high, low = split(zs[k])
        y = dot(m_ref[0], high) + (dot(m_ref[0], low) + dot(m_ref[1], high))
        index_x = k + factor * row
        signed_x = jnp.where(index_x < count // 2, index_x, index_x - count)
        wave_x = 2.0 * math.pi / (count * grid_step) * signed_x.astype(jnp.float32)
        vertical = rest - wave_x * wave_x
        size = jnp.sqrt(jnp.abs(vertical)) * depth_step
        damping = jnp.where(vertical < 0.0, jnp.exp(-size), 1.0) * (1.0 / (count * count))
        sn, cs = sin_cos(jnp.where(vertical > 0.0, size, 0.0) - flat)
        tr, ti = damping * cs, damping * sn
        re, im = y[:LANES], y[LANES:]
        z = jnp.concatenate([re * tr - im * ti, re * ti + im * tr], axis=0)
        high, low = split(z)
        zs[k] = dot(m_ref[2], high) + (dot(m_ref[2], low) + dot(m_ref[3], high))
        return carry

    lax.fori_loop(0, factor, product, 0)

    def tile_out(t, carry):
        r = pl.multiple_of(t * 8, 8)
        for lane in range(0, width, LANES):
            lanes = pl.ds(lane, LANES)
            cells = []
            for k in range(factor):
                re, im = zs[k, pl.ds(r, 8), lanes], zs[k, pl.ds(LANES + r, 8), lanes]
                if k:
                    c, s = tw_ref[0, k, pl.ds(r, 8), :], tw_ref[1, k, pl.ds(r, 8), :]
                    re, im = re * c - im * s, im * c + re * s
                cells.append((re, im))
            for n, (re, im) in enumerate(fft_list(cells, 1.0)):
                at = n * LANES
                rows = pl.ds(at % rows_in + r, 8)
                out_ref[at // rows_in, 0, rows, lanes] = re
                out_ref[at // rows_in, 1, rows, lanes] = im
        return carry

    lax.fori_loop(0, LANES // 8, tile_out, 0)
    for d in range(strips):
        for c in range(2):
            out_ref[d, c, pl.ds(rows_in, HALO), :] = jnp.zeros((HALO, width), jnp.float32)
            if d > 0:
                out_ref[d, c, pl.ds(rows_in, 1), :] = out_ref[d - 1, c, pl.ds(rows_in - 1, 1), :]
            if d < strips - 1:
                out_ref[d, c, pl.ds(rows_in + 1, 1), :] = out_ref[d + 1, c, pl.ds(0, 1), :]


def finish_kernel(
    ang_ref, mean_ref, in_ref, src_ref, slow_ref, tw_ref, m_ref, *rest, member, batch_total
):
    if member:
        _, before_ref, out_ref, term_ref, zs, field = rest
    else:
        out_ref, term_ref, zs, field = rest
    factor, tall = zs.shape[0], zs.shape[1]
    rows_in, width = tall - HALO, in_ref.shape[3]
    block, part_width = term_ref.shape[1:]
    full = field.shape[2]
    step = pl.program_id(0)

    @pl.when(step == 0)
    def _():
        for k in range(factor):
            at = k * LANES
            cols = pl.ds(at % width, LANES)
            x = jnp.concatenate(
                [in_ref[at // width, 0, :, cols], in_ref[at // width, 1, :, cols]], axis=1
            )
            high, low = split(x)
            zs[k] = dot(high, m_ref[0]) + (dot(low, m_ref[0]) + dot(high, m_ref[1]))

        def columns(rows):
            cells = []
            for k in range(factor):
                re, im = zs[k, rows, pl.ds(0, LANES)], zs[k, rows, pl.ds(LANES, LANES)]
                if k:
                    c, s = tw_ref[0, pl.ds(k, 1), :], tw_ref[1, pl.ds(k, 1), :]
                    re, im = re * c - im * s, im * c + re * s
                cells.append((re, im))
            return fft_list(cells, 1.0)

        def tile(t, carry):
            r = pl.multiple_of(t * 8, 8)
            for n, pair in enumerate(columns(pl.ds(r, 8))):
                for c in range(2):
                    field[c, pl.ds(8 + r, 8), pl.ds(n * LANES, LANES)] = pair[c]
            return carry

        lax.fori_loop(0, rows_in // 8, tile, 0)
        for n, pair in enumerate(columns(pl.ds(rows_in, 8))):
            for c in range(2):
                field[c, pl.ds(7, 1), pl.ds(n * LANES, LANES)] = pair[c][0:1]
                field[c, pl.ds(8 + rows_in, 1), pl.ds(n * LANES, LANES)] = pair[c][1:2]

    angular = ang_ref[member]
    ahead = 0.5 / (angular * mean_ref[0])
    column = lax.broadcasted_iota(jnp.int32, (block, full), 1)
    start = pl.multiple_of(step * block, 8)
    centre, laplace = [], []
    for c in range(2):
        cells = field[c, pl.ds(start, block + 16), :]
        mid = cells[8 : 8 + block]
        up = pltpu.roll(cells, 1, 0)[8 : 8 + block]
        down = pltpu.roll(cells, block + 15, 0)[8 : 8 + block]
        left = jnp.where(column == 0, 0.0, pltpu.roll(mid, 1, 1))
        right = jnp.where(column == full - 1, 0.0, pltpu.roll(mid, full - 1, 1))
        centre.append(mid)
        laplace.append(up + down + left + right - 4.0 * mid)
    slow = jnp.concatenate([slow_ref[p] for p in range(slow_ref.shape[0])], axis=1)
    gain = (ahead - 0.5 / (angular * slow)) * (depth_step / (grid_step * grid_step))
    new_re = centre[0] + gain * laplace[1]
    new_im = centre[1] - gain * laplace[0]
    out_ref[0, 0] = new_re
    out_ref[1, 0] = new_im
    term = (new_re * src_ref[0, 0] + new_im * src_ref[1, 0]) * (1.0 / math.sqrt(batch_total))
    for p in range(slow_ref.shape[0]):
        part = term[:, p * part_width : (p + 1) * part_width]
        term_ref[p] = part + before_ref[p] if member else part


def params():
    return pltpu.CompilerParams(vmem_limit_bytes=VMEM_BYTES)


def whole(array):
    zeros = (0,) * array.ndim
    return pl.BlockSpec(array.shape, lambda *_: zeros)


SMEM = pl.BlockSpec(memory_space=pltpu.SMEM)


def local(wavefield, source_field, slowness, freq_index):
    _, members, rows, full = wavefield.shape
    strips, groups = lax.axis_size("lat"), lax.axis_size("freq")
    width = full // strips
    factor = full // LANES
    part_width = full // groups
    count_x = rows * strips
    angular = 2.0 * math.pi * freq_step * freq_index.astype(jnp.float32)
    tw = twiddle(full)
    tw_row = jnp.asarray(tw)
    tw_x = jnp.asarray(np.ascontiguousarray(np.broadcast_to(tw[..., None], tw.shape + (LANES,))))
    right_fwd, right_inv = dft_tables(-1.0), dft_tables(1.0)
    m_fwd, m_inv = split_table(right_fwd), split_table(right_inv)
    m_both = jnp.concatenate(
        [split_table(np.ascontiguousarray(right_fwd.T)), split_table(np.ascontiguousarray(right_inv.T))]
    )
    copies = jnp.broadcast_to(slowness, (groups,) + slowness.shape)
    strip = lax.all_to_all(copies, "freq", split_axis=0, concat_axis=0, tiled=True)

    block = 64

    def forward(member):
        tall = rows + HALO if member == 0 else rows
        return pl.pallas_call(
            functools.partial(forward_kernel, member=member),
            grid=(rows // block,),
            in_specs=[
                SMEM,
                pl.BlockSpec((2, 1, block, full), lambda i: (0, member, i, 0)),
                pl.BlockSpec((groups, block, part_width), lambda i: (0, i, 0)),
                whole(tw_row),
                whole(m_fwd),
            ],
            out_specs=pl.BlockSpec((strips, 2, tall, width), lambda i: (0, 0, 0, 0)),
            out_shape=jax.ShapeDtypeStruct((strips, 2, tall, width), jnp.float32),
            scratch_shapes=[
                pltpu.VMEM((factor, block, 2 * LANES), jnp.float32),
                pltpu.VMEM((8, LANES), jnp.float32),
            ],
            compiler_params=params(),
            cost_estimate=pl.CostEstimate(
                flops=4_000_000_000, bytes_accessed=40_000_000, transcendentals=0
            ),
            name="forward",
        )(angular, wavefield, strip, tw_row, m_fwd)

    def shift(member, mean_slow, spectra):
        return pl.pallas_call(
            functools.partial(shift_kernel, member=member),
            grid=(1,),
            in_specs=[SMEM, SMEM, whole(spectra), whole(tw_x), whole(m_both)],
            out_specs=pl.BlockSpec((strips, 2, rows + HALO, width), lambda i: (0, 0, 0, 0)),
            out_shape=jax.ShapeDtypeStruct((strips, 2, rows + HALO, width), jnp.float32),
            scratch_shapes=[pltpu.VMEM((factor, 2 * LANES, width), jnp.float32)],
            compiler_params=params(),
            cost_estimate=pl.CostEstimate(
                flops=10_000_000_000, bytes_accessed=100_000_000, transcendentals=0
            ),
            name="shift",
        )(angular, mean_slow, spectra, tw_x, m_both)

    final_block = 32

    def finish(member, mean_slow, lines, before):
        strip_block = pl.BlockSpec((groups, final_block, part_width), lambda i: (0, i, 0))
        field_block = pl.BlockSpec((2, 1, final_block, full), lambda i: (0, member, i, 0))
        specs = [SMEM, SMEM, whole(lines), field_block, strip_block, whole(tw_row), whole(m_inv)]
        arrays = [angular, mean_slow, lines, source_field, strip, tw_row, m_inv]
        aliases = {}
        if member:
            aliases = {len(arrays): 0}
            specs += [pl.BlockSpec(memory_space=pl.ANY), strip_block]
            arrays += list(before)
        return pl.pallas_call(
            functools.partial(
                finish_kernel, member=member, batch_total=members * groups
            ),
            grid=(rows // final_block,),
            in_specs=specs,
            out_specs=[field_block, strip_block],
            out_shape=[
                jax.ShapeDtypeStruct((2, members, rows, full), jnp.float32),
                jax.ShapeDtypeStruct((groups, rows, part_width), jnp.float32),
            ],
            scratch_shapes=[
                pltpu.VMEM((factor, rows + HALO, 2 * LANES), jnp.float32),
                pltpu.VMEM((2, rows + 16, full), jnp.float32),
            ],
            input_output_aliases=aliases,
            compiler_params=params(),
            cost_estimate=pl.CostEstimate(
                flops=8_000_000_000, bytes_accessed=80_000_000, transcendentals=0
            ),
            name="finish",
        )(*arrays)

    def exchange(cells):
        return lax.all_to_all(cells, "lat", split_axis=0, concat_axis=0, tiled=True)

    spectra = [forward(m) for m in range(members)]
    lines = [exchange(s) for s in spectra]
    total = jnp.sum(lax.slice(lines[0], (0, 0, rows, 0), (strips, 1, rows + 1, 1)))
    mean_slow = (total / (count_x * full)).reshape(1)
    shifted = [exchange(shift(m, mean_slow, lines[m])) for m in range(members)]
    state = None
    for m in range(members):
        state = finish(m, mean_slow, shifted[m], state)
    field, terms = state
    image = jnp.sum(
        lax.all_to_all(terms, "freq", split_axis=0, concat_axis=0, tiled=True), axis=0
    )
    return (field, image)


def solution(mesh):
    return jax.shard_map(
        local,
        mesh=mesh,
        in_specs=(
            P(None, "freq", "lat", None),
            P(None, "freq", "lat", None),
            P("lat", "freq"),
            P("freq"),
        ),
        out_specs=(P(None, "freq", "lat", None), P("lat", "freq")),
        check_vma=False,
    )
```

```python
import functools
import math

import jax
import jax.numpy as jnp
import numpy as np
from jax import lax
from jax.experimental import pallas as pl
from jax.experimental.pallas import tpu as pltpu
from jax.sharding import PartitionSpec as P

depth_step = 10.0
grid_step = 25.0
freq_step = 0.0625
LANES = 128
HALO = 8
VMEM_BYTES = 48 * 1024 * 1024


def dft_tables(sign):
    i = np.arange(LANES)
    ang = 2.0 * math.pi / LANES * ((i[:, None] * i[None, :]) % LANES)
    c, s = np.cos(ang), sign * np.sin(ang)
    return np.block([[c, s], [-s, c]])


def split_table(table):
    high = jnp.asarray(table.astype(np.float32)).astype(jnp.bfloat16)
    high64 = np.asarray(table.astype(np.float32).astype(jnp.bfloat16)).astype(np.float64)
    low = (table - high64).astype(np.float32).astype(jnp.bfloat16)
    return jnp.stack([high, jnp.asarray(low)])


def twiddle(count):
    factor = count // LANES
    k, n = np.arange(factor), np.arange(LANES)
    ang = 2.0 * math.pi / count * ((k[:, None] * n[None, :]) % count)
    return np.stack([np.cos(ang), np.sin(ang)]).astype(np.float32)


def fft_list(values, sign):
    count = len(values)
    if count == 1:
        return values
    even, odd = fft_list(values[0::2], sign), fft_list(values[1::2], sign)
    low, high = [], []
    for k in range(count // 2):
        (er, ei), (r, i) = even[k], odd[k]
        if k == 0:
            tr, ti = r, i
        elif 4 * k == count:
            tr, ti = (-i, r) if sign > 0 else (i, -r)
        else:
            c = math.cos(2.0 * math.pi * k / count)
            s = sign * math.sin(2.0 * math.pi * k / count)
            if abs(abs(c) - abs(s)) < 1e-9:
                h = math.sqrt(0.5)
                sc, ss = (1 if c > 0 else -1), (1 if s > 0 else -1)
                tr = h * (r - i) if sc * ss > 0 else h * (r + i)
                ti = h * (i + r) if sc * ss > 0 else h * (i - r)
                if sc < 0:
                    tr, ti = -tr, -ti
            else:
                tr, ti = c * r - s * i, c * i + s * r
        low.append((er + tr, ei + ti))
        high.append((er - tr, ei - ti))
    return low + high


def sin_cos(angle):
    turns = jnp.round(angle * (0.5 / math.pi))
    r = angle - turns * 6.28125 - turns * (2.0 * math.pi - 6.28125)
    r2 = r * r
    s = jnp.full_like(r, 1.0 / math.factorial(17))
    for n in range(15, 0, -2):
        s = s * r2 + ((-1) ** (n // 2)) / math.factorial(n)
    c = jnp.full_like(r, -1.0 / math.factorial(18))
    for n in range(16, -1, -2):
        c = c * r2 + ((-1) ** (n // 2)) / math.factorial(n)
    return s * r, c


def split(x):
    high = x.astype(jnp.bfloat16)
    return high, (x - high.astype(jnp.float32)).astype(jnp.bfloat16)


def dot(a, b):
    return jnp.dot(a, b, preferred_element_type=jnp.float32)


def forward_kernel(ang_ref, wave_ref, slow_ref, tw_ref, m_ref, out_ref, zs, total, *, member):
    factor, block = zs.shape[0], zs.shape[1]
    part_width, width = slow_ref.shape[2], out_ref.shape[3]
    scale = ang_ref[member] * depth_step
    step = pl.program_id(0)
    start = pl.multiple_of(step * block, block)
    last = pl.num_programs(0) - 1

    @pl.when(step == 0)
    def _():
        total[...] = jnp.zeros_like(total)

    def tile(t, sums):
        rows = pl.ds(pl.multiple_of(t * 8, 8), 8)
        cells = []
        for n in range(factor):
            at = n * LANES
            s = slow_ref[at // part_width, rows, pl.ds(at % part_width, LANES)]
            sums = sums + s
            sn, cs = sin_cos(s * scale)
            re = wave_ref[0, 0, rows, pl.ds(at, LANES)]
            im = wave_ref[1, 0, rows, pl.ds(at, LANES)]
            cells.append((re * cs - im * sn, re * sn + im * cs))
        for k, (re, im) in enumerate(fft_list(cells, -1.0)):
            if k:
                c, s = tw_ref[0, pl.ds(k, 1), :], tw_ref[1, pl.ds(k, 1), :]
                re, im = re * c + im * s, im * c - re * s
            zs[k, rows, pl.ds(0, LANES)] = re
            zs[k, rows, pl.ds(LANES, LANES)] = im
        return sums

    total[...] = lax.fori_loop(0, block // 8, tile, total[...])
    for g in range(0, factor, 4):
        high, low = split(zs[pl.ds(g, 4)].reshape(4 * block, 2 * LANES))
        y = dot(high, m_ref[0]) + (dot(low, m_ref[0]) + dot(high, m_ref[1]))
        y = y.reshape(4, block, 2 * LANES)
        for j in range(4):
            at = (g + j) * LANES
            cols = pl.ds(at % width, LANES)
            out_ref[at // width, 0, pl.ds(start, block), cols] = y[j, :, :LANES]
            out_ref[at // width, 1, pl.ds(start, block), cols] = y[j, :, LANES:]

    if member == 0:
        @pl.when(step == last)
        def _():
            value = jnp.full((HALO, width), jnp.sum(total[...]), jnp.float32)
            for d in range(out_ref.shape[0]):
                for c in range(2):
                    out_ref[d, c, pl.ds(out_ref.shape[2] - HALO, HALO), :] = value


def shift_kernel(ang_ref, mean_ref, in_ref, tw_ref, m_ref, out_ref, zs, *, member):
    factor, width = zs.shape[0], zs.shape[2]
    strips, rows_in = in_ref.shape[0], out_ref.shape[2] - HALO
    count = factor * LANES
    base = lax.axis_index("lat") * width

    def tile_in(t, carry):
        r = pl.multiple_of(t * 8, 8)
        for lane in range(0, width, LANES):
            lanes = pl.ds(lane, LANES)
            cells = []
            for n in range(factor):
                at = n * LANES
                rows = pl.ds(at % rows_in + r, 8)
                cells.append(
                    (in_ref[at // rows_in, 0, rows, lanes], in_ref[at // rows_in, 1, rows, lanes])
                )
            for k, (re, im) in enumerate(fft_list(cells, -1.0)):
                if k:
                    c, s = tw_ref[0, k, pl.ds(r, 8), :], tw_ref[1, k, pl.ds(r, 8), :]
                    re, im = re * c + im * s, im * c - re * s
                zs[k, pl.ds(r, 8), lanes] = re
                zs[k, pl.ds(LANES + r, 8), lanes] = im
        return carry

    lax.fori_loop(0, LANES // 8, tile_in, 0)

    angular_mean = ang_ref[member] * mean_ref[0]
    flat = angular_mean * depth_step
    place = base + lax.broadcasted_iota(jnp.int32, (LANES, width), 1)
    index_y = place // LANES + factor * (place % LANES)
    signed_y = jnp.where(index_y < count // 2, index_y, index_y - count)
    wave_y = 2.0 * math.pi / (count * grid_step) * signed_y.astype(jnp.float32)
    rest = angular_mean * angular_mean - wave_y * wave_y
    row = lax.broadcasted_iota(jnp.int32, (LANES, width), 0)

    def product(k, carry):
        high, low = split(zs[k])
        y = dot(m_ref[0], high) + (dot(m_ref[0], low) + dot(m_ref[1], high))
        index_x = k + factor * row
        signed_x = jnp.where(index_x < count // 2, index_x, index_x - count)
        wave_x = 2.0 * math.pi / (count * grid_step) * signed_x.astype(jnp.float32)
        vertical = rest - wave_x * wave_x
        size = jnp.sqrt(jnp.abs(vertical)) * depth_step
        damping = jnp.where(vertical < 0.0, jnp.exp(-size), 1.0) * (1.0 / (count * count))
        sn, cs = sin_cos(jnp.where(vertical > 0.0, size, 0.0) - flat)
        tr, ti = damping * cs, damping * sn
        re, im = y[:LANES], y[LANES:]
        z = jnp.concatenate([re * tr - im * ti, re * ti + im * tr], axis=0)
        high, low = split(z)
        zs[k] = dot(m_ref[2], high) + (dot(m_ref[2], low) + dot(m_ref[3], high))
        return carry

    lax.fori_loop(0, factor, product, 0)

    def tile_out(t, carry):
        r = pl.multiple_of(t * 8, 8)
        for lane in range(0, width, LANES):
            lanes = pl.ds(lane, LANES)
            cells = []
            for k in range(factor):
                re, im = zs[k, pl.ds(r, 8), lanes], zs[k, pl.ds(LANES + r, 8), lanes]
                if k:
                    c, s = tw_ref[0, k, pl.ds(r, 8), :], tw_ref[1, k, pl.ds(r, 8), :]
                    re, im = re * c - im * s, im * c + re * s
                cells.append((re, im))
            for n, (re, im) in enumerate(fft_list(cells, 1.0)):
                at = n * LANES
                rows = pl.ds(at % rows_in + r, 8)
                out_ref[at // rows_in, 0, rows, lanes] = re
                out_ref[at // rows_in, 1, rows, lanes] = im
        return carry

    lax.fori_loop(0, LANES // 8, tile_out, 0)
    for d in range(strips):
        for c in range(2):
            out_ref[d, c, pl.ds(rows_in, HALO), :] = jnp.zeros((HALO, width), jnp.float32)
            if d > 0:
                out_ref[d, c, pl.ds(rows_in, 1), :] = out_ref[d - 1, c, pl.ds(rows_in - 1, 1), :]
            if d < strips - 1:
                out_ref[d, c, pl.ds(rows_in + 1, 1), :] = out_ref[d + 1, c, pl.ds(0, 1), :]


def finish_kernel(
    ang_ref, mean_ref, in_ref, src_ref, slow_ref, tw_ref, m_ref, *rest, member, batch_total
):
    if member:
        _, before_ref, out_ref, term_ref, zs, field = rest
    else:
        out_ref, term_ref, zs, field = rest
    factor, tall = zs.shape[0], zs.shape[1]
    rows_in, width = tall - HALO, in_ref.shape[3]
    block, part_width = term_ref.shape[1:]
    full = field.shape[2]
    step = pl.program_id(0)

    @pl.when(step == 0)
    def _():
        for k in range(factor):
            at = k * LANES
            cols = pl.ds(at % width, LANES)
            x = jnp.concatenate(
                [in_ref[at // width, 0, :, cols], in_ref[at // width, 1, :, cols]], axis=1
            )
            high, low = split(x)
            zs[k] = dot(high, m_ref[0]) + (dot(low, m_ref[0]) + dot(high, m_ref[1]))

        def columns(rows):
            cells = []
            for k in range(factor):
                re, im = zs[k, rows, pl.ds(0, LANES)], zs[k, rows, pl.ds(LANES, LANES)]
                if k:
                    c, s = tw_ref[0, pl.ds(k, 1), :], tw_ref[1, pl.ds(k, 1), :]
                    re, im = re * c - im * s, im * c + re * s
                cells.append((re, im))
            return fft_list(cells, 1.0)

        def tile(t, carry):
            r = pl.multiple_of(t * 8, 8)
            for n, pair in enumerate(columns(pl.ds(r, 8))):
                for c in range(2):
                    field[c, pl.ds(8 + r, 8), pl.ds(n * LANES, LANES)] = pair[c]
            return carry

        lax.fori_loop(0, rows_in // 8, tile, 0)
        for n, pair in enumerate(columns(pl.ds(rows_in, 8))):
            for c in range(2):
                field[c, pl.ds(7, 1), pl.ds(n * LANES, LANES)] = pair[c][0:1]
                field[c, pl.ds(8 + rows_in, 1), pl.ds(n * LANES, LANES)] = pair[c][1:2]

    angular = ang_ref[member]
    ahead = 0.5 / (angular * mean_ref[0])
    column = lax.broadcasted_iota(jnp.int32, (block, full), 1)
    start = pl.multiple_of(step * block, 8)
    centre, laplace = [], []
    for c in range(2):
        cells = field[c, pl.ds(start, block + 16), :]
        mid = cells[8 : 8 + block]
        up = pltpu.roll(cells, 1, 0)[8 : 8 + block]
        down = pltpu.roll(cells, block + 15, 0)[8 : 8 + block]
        left = jnp.where(column == 0, 0.0, pltpu.roll(mid, 1, 1))
        right = jnp.where(column == full - 1, 0.0, pltpu.roll(mid, full - 1, 1))
        centre.append(mid)
        laplace.append(up + down + left + right - 4.0 * mid)
    slow = jnp.concatenate([slow_ref[p] for p in range(slow_ref.shape[0])], axis=1)
    gain = (ahead - 0.5 / (angular * slow)) * (depth_step / (grid_step * grid_step))
    new_re = centre[0] + gain * laplace[1]
    new_im = centre[1] - gain * laplace[0]
    out_ref[0, 0] = new_re
    out_ref[1, 0] = new_im
    term = (new_re * src_ref[0, 0] + new_im * src_ref[1, 0]) * (1.0 / math.sqrt(batch_total))
    for p in range(slow_ref.shape[0]):
        part = term[:, p * part_width : (p + 1) * part_width]
        term_ref[p] = part + before_ref[p] if member else part


def params():
    return pltpu.CompilerParams(vmem_limit_bytes=VMEM_BYTES)


def whole(array):
    zeros = (0,) * array.ndim
    return pl.BlockSpec(array.shape, lambda *_: zeros)


SMEM = pl.BlockSpec(memory_space=pltpu.SMEM)


def local(wavefield, source_field, slowness, freq_index):
    _, members, rows, full = wavefield.shape
    strips, groups = lax.axis_size("lat"), lax.axis_size("freq")
    width = full // strips
    factor = full // LANES
    part_width = full // groups
    count_x = rows * strips
    angular = 2.0 * math.pi * freq_step * freq_index.astype(jnp.float32)
    tw = twiddle(full)
    tw_row = jnp.asarray(tw)
    tw_x = jnp.asarray(np.ascontiguousarray(np.broadcast_to(tw[..., None], tw.shape + (LANES,))))
    right_fwd, right_inv = dft_tables(-1.0), dft_tables(1.0)
    m_fwd, m_inv = split_table(right_fwd), split_table(right_inv)
    m_both = jnp.concatenate(
        [split_table(np.ascontiguousarray(right_fwd.T)), split_table(np.ascontiguousarray(right_inv.T))]
    )
    copies = jnp.broadcast_to(slowness, (groups,) + slowness.shape)
    strip = lax.all_to_all(copies, "freq", split_axis=0, concat_axis=0, tiled=True)

    block = 128

    def forward(member):
        tall = rows + HALO if member == 0 else rows
        return pl.pallas_call(
            functools.partial(forward_kernel, member=member),
            grid=(rows // block,),
            in_specs=[
                SMEM,
                pl.BlockSpec((2, 1, block, full), lambda i: (0, member, i, 0)),
                pl.BlockSpec((groups, block, part_width), lambda i: (0, i, 0)),
                whole(tw_row),
                whole(m_fwd),
            ],
            out_specs=pl.BlockSpec((strips, 2, tall, width), lambda i: (0, 0, 0, 0)),
            out_shape=jax.ShapeDtypeStruct((strips, 2, tall, width), jnp.float32),
            scratch_shapes=[
                pltpu.VMEM((factor, block, 2 * LANES), jnp.float32),
                pltpu.VMEM((8, LANES), jnp.float32),
            ],
            compiler_params=params(),
            cost_estimate=pl.CostEstimate(
                flops=4_000_000_000, bytes_accessed=40_000_000, transcendentals=0
            ),
            name="forward",
        )(angular, wavefield, strip, tw_row, m_fwd)

    def shift(member, mean_slow, spectra):
        return pl.pallas_call(
            functools.partial(shift_kernel, member=member),
            grid=(1,),
            in_specs=[SMEM, SMEM, whole(spectra), whole(tw_x), whole(m_both)],
            out_specs=pl.BlockSpec((strips, 2, rows + HALO, width), lambda i: (0, 0, 0, 0)),
            out_shape=jax.ShapeDtypeStruct((strips, 2, rows + HALO, width), jnp.float32),
            scratch_shapes=[pltpu.VMEM((factor, 2 * LANES, width), jnp.float32)],
            compiler_params=params(),
            cost_estimate=pl.CostEstimate(
                flops=10_000_000_000, bytes_accessed=100_000_000, transcendentals=0
            ),
            name="shift",
        )(angular, mean_slow, spectra, tw_x, m_both)

    final_block = 64

    def finish(member, mean_slow, lines, before):
        strip_block = pl.BlockSpec((groups, final_block, part_width), lambda i: (0, i, 0))
        field_block = pl.BlockSpec((2, 1, final_block, full), lambda i: (0, member, i, 0))
        specs = [SMEM, SMEM, whole(lines), field_block, strip_block, whole(tw_row), whole(m_inv)]
        arrays = [angular, mean_slow, lines, source_field, strip, tw_row, m_inv]
        aliases = {}
        if member:
            aliases = {len(arrays): 0}
            specs += [pl.BlockSpec(memory_space=pl.ANY), strip_block]
            arrays += list(before)
        return pl.pallas_call(
            functools.partial(
                finish_kernel, member=member, batch_total=members * groups
            ),
            grid=(rows // final_block,),
            in_specs=specs,
            out_specs=[field_block, strip_block],
            out_shape=[
                jax.ShapeDtypeStruct((2, members, rows, full), jnp.float32),
                jax.ShapeDtypeStruct((groups, rows, part_width), jnp.float32),
            ],
            scratch_shapes=[
                pltpu.VMEM((factor, rows + HALO, 2 * LANES), jnp.float32),
                pltpu.VMEM((2, rows + 16, full), jnp.float32),
            ],
            input_output_aliases=aliases,
            compiler_params=params(),
            cost_estimate=pl.CostEstimate(
                flops=8_000_000_000, bytes_accessed=80_000_000, transcendentals=0
            ),
            name="finish",
        )(*arrays)

    def exchange(cells):
        return lax.all_to_all(cells, "lat", split_axis=0, concat_axis=0, tiled=True)

    spectra = [forward(m) for m in range(members)]
    lines = [exchange(s) for s in spectra]
    total = jnp.sum(lax.slice(lines[0], (0, 0, rows, 0), (strips, 1, rows + 1, 1)))
    mean_slow = (total / (count_x * full)).reshape(1)
    shifted = [exchange(shift(m, mean_slow, lines[m])) for m in range(members)]
    state = None
    for m in range(members):
        state = finish(m, mean_slow, shifted[m], state)
    field, terms = state
    image = jnp.sum(
        lax.all_to_all(terms, "freq", split_axis=0, concat_axis=0, tiled=True), axis=0
    )
    return (field, image)


def solution(mesh):
    return jax.shard_map(
        local,
        mesh=mesh,
        in_specs=(
            P(None, "freq", "lat", None),
            P(None, "freq", "lat", None),
            P("lat", "freq"),
            P("freq"),
        ),
        out_specs=(P(None, "freq", "lat", None), P("lat", "freq")),
        check_vma=False,
    )
```
